256 devices in a mesh: row: 32 (over z, y), col: 8 (over x, core).
Axes of the slice: x: 4, y: 4, z: 8, core: 2. Of those that a mesh axis runs over, the one named last changes fastest.
Arguments:
- tokens: bfloat16 [4096, 5120], P('row', 'col'), may hold values from -6 to 6
- target: bfloat16 [4096, 5120], P('row', 'col'), may hold values from -6 to 6
- w_gate: bfloat16 [5120, 13824], P('col', 'row'), may hold values from -0.078125 to 0.078125
- w_up: bfloat16 [5120, 13824], P('col', 'row'), may hold values from -0.078125 to 0.078125
- w_down: bfloat16 [13824, 5120], P('row', 'col'), may hold values from -0.0546875 to 0.0546875
- factor_u: bfloat16 [5120, 256], P('col'), may hold values from -0.078125 to 0.078125
- factor_v: bfloat16 [256, 13824], P(None, 'row'), may hold values from -3 to 3
Outputs:
- mixed: bfloat16 [4096, 5120], P('row', 'col')
- fitness: float32 [64], replicated
- update: float32 [5120, 13824], P('col', 'row')
The draws below stay inside these ranges and needn't reach their ends.
All inputs are finite; a program needn't handle non-finite values.
Results may differ from the reference program's by a relative error of at most 0.0049.
Values may be sent and summed in bfloat16 or wider, within the bound.
No kernel may reach another device: no remote copies, remote signals or barrier semaphores. Data moves between devices by JAX's collectives and lax.ppermute only.
A program may use at most 128 MiB of HBM per device.

```python
import math
import jax
import jax.numpy as jnp
from jax import lax

D = 5120
FF = 13824
RANK = 4
SEQ = 64
MEMBERS = 64
TOKENS = 4096


def shard_levels(stream_key, extent, shards, smallest, top_value):
    gain, own = 1.0, jax.random.fold_in(stream_key, 6)
    for dim, shards_of in shards:
        draws = jnp.exp(jax.random.uniform(jax.random.fold_in(own, dim), (shards_of,), jnp.float32, smallest / len(shards), top_value / len(shards)))
        gain = gain * jnp.repeat(draws, extent[dim] // shards_of).reshape([-1 if axis == dim else 1 for axis in range(len(extent))])
    return gain


def centred(own_key, extent, spread, bound, shards=(), dtype=jnp.bfloat16):
    gain = shard_levels(own_key, extent, shards, -0.22, 0.18) if shards else 1.0
    drawn = jax.random.normal(own_key, extent, jnp.float32) * spread * gain
    return jnp.minimum(jnp.maximum(drawn, -bound), bound).astype(dtype)


def setup_inputs(seed: int = 0) -> dict:
    keys = jax.random.split(jax.random.key(seed), 8)
    tokens = centred(keys[0], (TOKENS, D), 1.0, 6.0, ((0, 32), (1, 8)))
    target = centred(keys[1], (TOKENS, D), 1.0, 6.0, ((0, 32), (1, 8)))
    w_gate = centred(keys[2], (D, FF), D ** -0.5, 0.078125, ((0, 8), (1, 32)))
    w_up = centred(keys[3], (D, FF), D ** -0.5, 0.078125, ((0, 8), (1, 32)))
    w_down = centred(keys[4], (FF, D), FF ** -0.5, 0.0546875, ((0, 32), (1, 8)))
    factor_u = centred(keys[5], (D, MEMBERS * RANK), D ** -0.5, 0.078125, ((0, 8),))
    factor_v = centred(keys[6], (MEMBERS * RANK, FF), RANK ** -0.5, 3.0, ((1, 32),))
    return dict(tokens=tokens, target=target, w_gate=w_gate, w_up=w_up, w_down=w_down, factor_u=factor_u, factor_v=factor_v)


sigma_scale = 0.5

def reference(tokens, target, w_gate, w_up, w_down, factor_u, factor_v):
    gate = jnp.dot(tokens, w_gate, preferred_element_type=jnp.float32)
    up = jnp.dot(tokens, w_up, preferred_element_type=jnp.float32)
    grouped = tokens.reshape(MEMBERS, SEQ, D).astype(jnp.float32)
    u_three = factor_u.reshape(D, MEMBERS, RANK).astype(jnp.float32)
    v_three = factor_v.reshape(MEMBERS, RANK, FF).astype(jnp.float32)
    low = jnp.einsum('psd,dpr->psr', grouped, u_three, precision=lax.Precision.HIGHEST)
    corr = jnp.einsum('psr,prf->psf', low, v_three, precision=lax.Precision.HIGHEST).reshape(TOKENS, FF)
    up = up + sigma_scale * corr
    hidden = (jax.nn.silu(gate) * up).astype(jnp.bfloat16)
    out = jnp.dot(hidden, w_down, preferred_element_type=jnp.float32)
    mixed = out.astype(jnp.bfloat16)
    prod = (out * target.astype(jnp.float32)).reshape(MEMBERS, SEQ * D)
    fitness = lax.optimization_barrier(jnp.sum(prod, axis=1)) / math.sqrt(SEQ * D)
    weights = jnp.repeat(fitness, RANK)
    update = jnp.dot(factor_u.astype(jnp.float32) * weights[None, :], factor_v.astype(jnp.float32), precision=lax.Precision.HIGHEST, preferred_element_type=jnp.float32) * math.sqrt(D / MEMBERS)
    return (mixed, fitness, update)
```

```python
import math

import jax
import jax.numpy as jnp
from jax import lax
from jax.sharding import Mesh
from jax.sharding import PartitionSpec as P

D = 5120
RANK = 4
SEQ = 64
SIGMA = 0.5

Z, Y, X, C = 8, 4, 4, 2
ROW = ("z", "y")
COL = ("x", "core")
SIZES = {"z": Z, "y": Y, "x": X, "core": C}
F32 = jnp.float32
BF16 = jnp.bfloat16


def shift(value, axis, step):
    n = SIZES[axis]
    return lax.ppermute(value, axis, [(i, (i + step) % n) for i in range(n)])


def ring_gather(value, axis):
    n = SIZES[axis]
    half = n // 2
    blocks = [None] * n
    blocks[0] = value
    right = left = value
    for step in range(1, half):
        right = shift(right, axis, 1)
        left = shift(left, axis, -1)
        blocks[n - step] = right
        blocks[step] = left
    mid = value.shape[1] // 2
    right = shift(right[:, :mid], axis, 1)
    left = shift(left[:, mid:], axis, -1)
    blocks[half] = jnp.concatenate([right, left], axis=1)
    return jnp.concatenate(blocks, axis=0)


def ring_scatter(value, axis):
    n = SIZES[axis]
    half = n // 2
    rows = value.shape[0] // n
    mid = value.shape[1] // 2
    blocks = [value[d * rows : (d + 1) * rows] for d in range(n)]
    ahead = shift(blocks[half][:, :mid].astype(BF16), axis, 1).astype(F32)
    behind = shift(blocks[half][:, mid:].astype(BF16), axis, -1).astype(F32)
    pad = ((0, 0), (0, value.shape[1] - mid)), ((0, 0), (mid, 0))
    ahead = jnp.pad(ahead, pad[0])
    behind = jnp.pad(behind, pad[1])
    for step in range(half - 1, 0, -1):
        ahead = shift((ahead + blocks[step]).astype(BF16), axis, 1).astype(F32)
        behind = shift((behind + blocks[n - step]).astype(BF16), axis, -1).astype(F32)
    return ahead + behind + blocks[0]


def split_two(value):
    high = value.astype(BF16)
    return high, (value - high.astype(F32)).astype(BF16)


def body(tokens, target, w_gate, w_up, w_down, factor_u, factor_v):
    dev_rows, dev_feat = tokens.shape
    members = factor_u.shape[1] // RANK
    units = w_up.shape[1]
    model = dev_feat * X * C
    own = dev_rows // (X * C)
    half = own // 2
    z, y = lax.axis_index("z"), lax.axis_index("y")
    x, core = lax.axis_index("x"), lax.axis_index("core")

    def to_rows(value):
        moved = lax.all_to_all(value.reshape(X * C, own, dev_feat), COL, 0, 0, tiled=True)
        return jnp.swapaxes(moved, 0, 1).reshape(own, model)

    mine = to_rows(tokens)
    goal = to_rows(target)

    gate_w = lax.all_gather(w_gate, COL, axis=0, tiled=True)
    up_w = lax.all_gather(w_up, COL, axis=0, tiled=True)
    low_w = lax.all_gather(factor_u, COL, axis=0, tiled=True)
    down_w = lax.all_gather(w_down, COL, axis=0, tiled=False)
    v_twice = jnp.concatenate([factor_v, factor_v], axis=0)

    first = ring_gather(ring_gather(mine[:half], "y"), "z")
    second = ring_gather(ring_gather(mine[half:], "z"), "y")

    row = lax.broadcasted_iota(jnp.int32, (Z * Y * half, members * RANK), 0) // half
    column = lax.broadcasted_iota(jnp.int32, (Z * Y * half, members * RANK), 1) // RANK

    def member_of(dz, dy):
        return (((z + dz) % Z) * Y + (y + dy) % Y) * (dev_rows // SEQ) + (x * C + core) * own // SEQ

    def layer(block, member):
        gate = jnp.dot(block, gate_w, preferred_element_type=F32)
        low = jnp.dot(block, low_w, preferred_element_type=F32)
        low = jnp.where(column == member, low, 0.0)
        corr = jnp.dot(jnp.concatenate(split_two(low), axis=1), v_twice, preferred_element_type=F32)
        up = jnp.dot(block, up_w, preferred_element_type=F32) + SIGMA * corr
        hidden = (jax.nn.silu(gate) * up).astype(BF16)
        out = jnp.einsum("tk,nkf->tnf", hidden, down_w, preferred_element_type=F32)
        return out.reshape(block.shape[0], model)

    out_first = layer(first, member_of(row // Y, row % Y))
    out_second = layer(second, member_of(row % Z, row // Z))
    out = jnp.concatenate(
        [
            ring_scatter(ring_scatter(out_first, "z"), "y"),
            ring_scatter(ring_scatter(out_second, "y"), "z"),
        ],
        axis=0,
    )

    back = jnp.swapaxes(out.astype(BF16).reshape(own, X * C, dev_feat), 0, 1)
    mixed = lax.all_to_all(back, COL, 0, 0, tiled=True).reshape(dev_rows, dev_feat)

    score = jnp.sum(out * goal.astype(F32)) / math.sqrt(SEQ * D)
    parts = SEQ // own
    place = (z * Y + y) * X * C + x * C + core
    slots = lax.broadcasted_iota(jnp.int32, (members, parts), 0) * parts
    slots = slots + lax.broadcasted_iota(jnp.int32, (members, parts), 1)
    table = jnp.where(slots == place, score, 0.0)
    for axis in ("core", "x", "y", "z"):
        table = sum([shift(table, axis, step) for step in range(1, SIZES[axis])], table)
    fitness = jnp.sum(table, axis=1)

    weights = jnp.repeat(fitness, RANK) * math.sqrt(D / members)
    scaled = jnp.concatenate(split_two(factor_u.astype(F32) * weights[None, :]), axis=1)
    update = jnp.dot(scaled, v_twice, preferred_element_type=F32)
    return (mixed, fitness, update)


def solution(mesh):
    fine = Mesh(mesh.devices.reshape(Z, Y, X, C), ("z", "y", "x", "core"))
    return jax.shard_map(
        body,
        mesh=fine,
        in_specs=(
            P(ROW, COL),
            P(ROW, COL),
            P(COL, ROW),
            P(COL, ROW),
            P(ROW, COL),
            P(COL, None),
            P(None, ROW),
        ),
        out_specs=(P(ROW, COL), P(), P(COL, ROW)),
        check_vma=False,
    )
```

```python
import math

import jax
import jax.numpy as jnp
from jax import lax
from jax.sharding import Mesh
from jax.sharding import PartitionSpec as P

D = 5120
RANK = 4
SEQ = 64
SIGMA = 0.5
LANES = 128

Z, Y, X, C = 8, 4, 4, 2
ROW = ("z", "y")
COL = ("x", "core")
PLANE = ("y", "x", "core")
ALL = ("z", "y", "x", "core")
F32 = jnp.float32
BF16 = jnp.bfloat16


def shift(value, step):
    return lax.ppermute(value, "z", [(i, (i + step) % Z) for i in range(Z)])


def ring_gather(chunks):
    half = Z // 2
    blocks = [[chunk] + [None] * (Z - 1) for chunk in chunks]
    ends = [[chunk, chunk] for chunk in chunks]
    for step in range(1, half + 1):
        for k, end in enumerate(ends):
            if step < half or k % 2 == 0:
                end[0] = shift(end[0], 1)
                blocks[k][Z - step] = end[0]
            if step < half or k % 2 == 1:
                end[1] = shift(end[1], -1)
                blocks[k][step] = end[1]
    return blocks


def ring_scatter(chunks):
    half = Z // 2
    ends = [[None, None] for _ in chunks]
    for step in range(half, 0, -1):
        for k, blocks in enumerate(chunks):
            for side, sign in ((0, 1), (1, -1)):
                if step == half and side != k % 2:
                    continue
                send = blocks[(sign * step) % Z]
                if ends[k][side] is not None:
                    send = send + ends[k][side]
                ends[k][side] = shift(send.astype(BF16), sign).astype(F32)
    return [blocks[0] + end[0] + end[1] for blocks, end in zip(chunks, ends)]


def split_two(value):
    high = value.astype(BF16)
    return high, (value - high.astype(F32)).astype(BF16)


def body(tokens, target, w_gate, w_up, w_down, factor_u, factor_v):
    dev_rows, dev_feat = tokens.shape
    members = factor_u.shape[1] // RANK
    units = w_up.shape[1]
    cols = X * C
    model = dev_feat * cols
    own = dev_rows // cols
    local = dev_rows // SEQ
    z, y = lax.axis_index("z"), lax.axis_index("y")
    x, core = lax.axis_index("x"), lax.axis_index("core")

    weights = lax.all_gather(
        jnp.concatenate([w_down.T, w_gate, w_up], axis=1), COL, axis=0, tiled=True
    )
    v_twice = jnp.concatenate([factor_v, factor_v], axis=0)

    first = (z * Y + y) * local * RANK
    u_own = lax.dynamic_slice(factor_u, (0, first), (dev_feat, local * RANK))
    low = jnp.dot(tokens, u_own, preferred_element_type=F32)
    low = low.reshape(local, SEQ, local, RANK)
    low = jnp.concatenate([low[m, :, m] for m in range(local)], axis=0)
    extra = jnp.concatenate(split_two(low), axis=1)
    extra = jnp.pad(extra, ((0, 0), (0, LANES - extra.shape[1])))
    wide = jnp.concatenate([tokens, extra], axis=1).reshape(1, cols, own, dev_feat + LANES)
    wide = jnp.broadcast_to(wide, (Y, cols, own, dev_feat + LANES))
    moved = lax.all_to_all(wide.reshape(Y * cols, own, dev_feat + LANES), PLANE, 0, 0, tiled=True)
    moved = moved.reshape(Y, cols, own, dev_feat + LANES)
    part = moved[..., dev_feat:].astype(F32)
    part = part[..., :RANK] + part[..., RANK : 2 * RANK]
    extra = jnp.concatenate(split_two(jnp.sum(part, axis=1)), axis=-1)
    extra = jnp.pad(extra, ((0, 0), (0, 0), (0, LANES - extra.shape[-1])))
    rows = jnp.swapaxes(moved[..., :dev_feat], 1, 2).reshape(Y, own, model)
    rows = jnp.concatenate([rows, extra], axis=2).reshape(Y * own, model + LANES)
    plane = Y * own
    mid = plane // 2

    gathered = ring_gather([rows[:mid], rows[mid:]])
    every = jnp.concatenate(gathered[0] + gathered[1], axis=0)

    row = lax.broadcasted_iota(jnp.int32, (Z * plane, members * RANK * 2), 0)
    column = lax.broadcasted_iota(jnp.int32, (Z * plane, members * RANK * 2), 1)
    row_y = row // (Z * mid) * (Y // 2) + row % mid // own
    row_z = (z + row // mid) % Z
    member = (row_z * Y + row_y) * local + (x * C + core) * own // SEQ
    spread_row = lax.broadcasted_iota(jnp.int32, (LANES, members * RANK * 2), 0)
    spread_col = lax.broadcasted_iota(jnp.int32, (LANES, members * RANK * 2), 1)
    spread = spread_col // (members * RANK) * RANK + spread_col % RANK == spread_row
    low = jnp.dot(every[:, model:], spread.astype(BF16), preferred_element_type=F32)
    low = jnp.where(column % (members * RANK) // RANK == member, low, 0.0).astype(BF16)
    corr = jnp.dot(low, v_twice, preferred_element_type=F32)

    both = jnp.dot(every[:, :model], weights, preferred_element_type=F32)
    gate, up = both[:, units : 2 * units], both[:, 2 * units :] + SIGMA * corr
    hidden = (jax.nn.silu(gate) * up).astype(BF16)
    hidden, weights = lax.optimization_barrier((hidden, weights))
    out = lax.dot_general(
        hidden, weights[:, :units], (((1,), (1,)), ((), ())), preferred_element_type=F32
    )
    out = out.reshape(2, Z, mid, model)
    sums = ring_scatter([[out[k, d] for d in range(Z)] for k in range(2)])
    back = jnp.concatenate([s.astype(BF16) for s in sums], axis=0).reshape(Y, own, cols, dev_feat)
    back = jnp.swapaxes(back, 1, 2).reshape(Y * cols, own, dev_feat)
    back = lax.all_to_all(back, PLANE, 0, 0, tiled=True).reshape(Y, dev_rows, dev_feat)
    final = jnp.sum(back.astype(F32), axis=0)
    mixed = final.astype(BF16)

    score = jnp.sum((final * target.astype(F32)).reshape(local, SEQ, dev_feat), axis=(1, 2))
    score = jnp.pad(score / math.sqrt(SEQ * D), (0, LANES - local))
    devices = Z * Y * cols
    scores = lax.all_to_all(
        jnp.broadcast_to(score, (devices, 1, LANES)), ALL, 0, 0, tiled=True
    )
    scores = scores.reshape(Z * Y, cols, LANES)[:, :, :local]
    fitness = jnp.sum(scores, axis=1).reshape(members)

    scale = jnp.repeat(fitness, RANK) * math.sqrt(D / members)
    scaled = jnp.concatenate(split_two(factor_u.astype(F32) * scale[None, :]), axis=1)
    update = jnp.dot(scaled, v_twice, preferred_element_type=F32)
    return (mixed, fitness, update)


def solution(mesh):
    fine = Mesh(mesh.devices.reshape(Z, Y, X, C), ALL)
    return jax.shard_map(
        body,
        mesh=fine,
        in_specs=(
            P(ROW, COL),
            P(ROW, COL),
            P(COL, ROW),
            P(COL, ROW),
            P(ROW, COL),
            P(COL, None),
            P(None, ROW),
        ),
        out_specs=(P(ROW, COL), P(), P(COL, ROW)),
        check_vma=False,
    )
```

```python
import math

import jax
import jax.numpy as jnp
from jax import lax
from jax.sharding import Mesh
from jax.sharding import PartitionSpec as P

D = 5120
RANK = 4
SEQ = 64
SIGMA = 0.5
LANES = 128

Z, Y, X, C = 8, 4, 4, 2
ROW = ("z", "y")
COL = ("x", "core")
PLANE = ("y", "x", "core")
ALL = ("z", "y", "x", "core")
F32 = jnp.float32
BF16 = jnp.bfloat16


def shift(value, step):
    return lax.ppermute(value, "z", [(i, (i + step) % Z) for i in range(Z)])


def ring_gather(chunks):
    half = Z // 2
    rows = chunks[0].shape[0]
    total = jnp.zeros((len(chunks), Z) + chunks[0].shape, chunks[0].dtype)
    ends = [[chunk, chunk] for chunk in chunks]
    landed = [(k, 0, chunk) for k, chunk in enumerate(chunks)]
    for step in range(1, half + 1):
        coming = []
        for k, end in enumerate(ends):
            if step < half or k % 2 == 0:
                end[0] = shift(end[0], 1)
                coming.append((k, Z - step, end[0]))
            if step < half or k % 2 == 1:
                end[1] = shift(end[1], -1)
                coming.append((k, step, end[1]))
        for k, place, block in landed:
            total = total.at[k, place].set(block)
        if step < half:
            total, ends[0] = lax.optimization_barrier((total, ends[0]))
        landed = coming
    for k, place, block in landed:
        total = total.at[k, place].set(block)
    return total.reshape(len(chunks) * Z * rows, -1)


def ring_scatter(chunks):
    half = Z // 2
    ends = {}
    for step in range(half, 0, -1):
        sends = {}
        for k, blocks in enumerate(chunks):
            for side, sign in ((0, 1), (1, -1)):
                if step == half and side != k % 2:
                    continue
                block = blocks((sign * step) % Z)
                if (k, sign) in ends:
                    block = block + ends[k, sign]
                else:
                    block = lax.optimization_barrier(block)
                sends[k, sign] = block.astype(BF16)
        sends = lax.optimization_barrier(sends)
        ends = {key: shift(value, key[1]).astype(F32) for key, value in sends.items()}
    return [blocks(0) + ends[k, 1] + ends[k, -1] for k, blocks in enumerate(chunks)]


def split_two(value):
    high = value.astype(BF16)
    return high, (value - high.astype(F32)).astype(BF16)


def body(tokens, target, w_gate, w_up, w_down, factor_u, factor_v):
    dev_rows, dev_feat = tokens.shape
    members = factor_u.shape[1] // RANK
    units = w_up.shape[1]
    cols = X * C
    model = dev_feat * cols
    own = dev_rows // cols
    local = dev_rows // SEQ
    z, y = lax.axis_index("z"), lax.axis_index("y")
    x, core = lax.axis_index("x"), lax.axis_index("core")

    weights = lax.all_gather(
        jnp.concatenate([w_down.T, w_gate, w_up], axis=1), COL, axis=0, tiled=True
    )
    v_twice = jnp.concatenate([factor_v, factor_v], axis=0)

    first = (z * Y + y) * local * RANK
    u_own = lax.dynamic_slice(factor_u, (0, first), (dev_feat, local * RANK))
    low = jnp.dot(tokens, u_own, preferred_element_type=F32)
    low = low.reshape(local, SEQ, local, RANK)
    low = jnp.concatenate([low[m, :, m] for m in range(local)], axis=0)
    extra = jnp.concatenate(split_two(low), axis=1)
    extra = jnp.pad(extra, ((0, 0), (0, LANES - extra.shape[1])))
    wide = jnp.concatenate([tokens, extra], axis=1).reshape(1, cols, own, dev_feat + LANES)
    wide = jnp.broadcast_to(wide, (Y, cols, own, dev_feat + LANES))
    moved = lax.all_to_all(wide.reshape(Y * cols, own, dev_feat + LANES), PLANE, 0, 0, tiled=True)
    target, moved = lax.optimization_barrier((target, moved))
    goal = jnp.broadcast_to(target.reshape(1, cols, own, dev_feat), (Y, cols, own, dev_feat))
    goal = lax.all_to_all(goal.reshape(Y * cols, own, dev_feat), PLANE, 0, 0, tiled=True)
    goal = jnp.swapaxes(goal.reshape(Y, cols, own, dev_feat), 1, 2).reshape(Y, own, model)
    moved = moved.reshape(Y, cols, own, dev_feat + LANES)
    part = moved[..., dev_feat:].astype(F32)
    part = part[..., :RANK] + part[..., RANK : 2 * RANK]
    extra = jnp.concatenate(split_two(jnp.sum(part, axis=1)), axis=-1)
    extra = jnp.pad(extra, ((0, 0), (0, 0), (0, LANES - extra.shape[-1])))
    rows = jnp.swapaxes(moved[..., :dev_feat], 1, 2).reshape(Y, own, model)
    rows = jnp.concatenate([rows, extra], axis=2).reshape(Y * own, model + LANES)
    plane = Y * own
    mid = plane // 2

    every = ring_gather([rows[:mid], rows[mid:]])

    row = lax.broadcasted_iota(jnp.int32, (Z * plane, members * RANK * 2), 0)
    column = lax.broadcasted_iota(jnp.int32, (Z * plane, members * RANK * 2), 1)
    row_y = row // (Z * mid) * (Y // 2) + row % mid // own
    row_z = (z + row // mid) % Z
    member = (row_z * Y + row_y) * local + (x * C + core) * own // SEQ
    spread_row = lax.broadcasted_iota(jnp.int32, (LANES, members * RANK * 2), 0)
    spread_col = lax.broadcasted_iota(jnp.int32, (LANES, members * RANK * 2), 1)
    spread = spread_col // (members * RANK) * RANK + spread_col % RANK == spread_row
    low = jnp.dot(every[:, model:], spread.astype(BF16), preferred_element_type=F32)
    low = jnp.where(column % (members * RANK) // RANK == member, low, 0.0).astype(BF16)
    corr = jnp.dot(low, v_twice, preferred_element_type=F32)

    both = jnp.dot(every[:, :model], weights, preferred_element_type=F32)
    gate, up = both[:, units : 2 * units], both[:, 2 * units :] + SIGMA * corr
    hidden = (jax.nn.silu(gate) * up).astype(BF16)
    hidden, weights = lax.optimization_barrier((hidden, weights))
    out = lax.dot_general(
        hidden, weights[:, :units], (((1,), (1,)), ((), ())), preferred_element_type=F32
    )
    out = out.reshape(2, Z, mid, model)
    sums = ring_scatter([lambda d: out[0, d], lambda d: out[1, d]])
    total = jnp.concatenate(sums, axis=0).reshape(Y, own, model)
    back = jnp.swapaxes(total.astype(BF16).reshape(Y, own, cols, dev_feat), 1, 2)
    back = back.reshape(Y * cols, own, dev_feat)
    back = lax.all_to_all(back, PLANE, 0, 0, tiled=True).reshape(Y, dev_rows, dev_feat)
    mixed = jnp.sum(back.astype(F32), axis=0).astype(BF16)

    score = jnp.sum(total * goal.astype(F32), axis=(1, 2)) / math.sqrt(SEQ * D)
    score = jnp.pad(score, (0, LANES - Y))
    devices = Z * Y * cols
    scores = lax.all_to_all(
        jnp.broadcast_to(score, (devices, 1, LANES)), ALL, 0, 0, tiled=True
    )
    scores = scores.reshape(Z, Y, local, cols // local, LANES)[..., :Y]
    fitness = jnp.swapaxes(jnp.sum(scores, axis=(1, 3)), 1, 2).reshape(members)

    scale = jnp.repeat(fitness, RANK) * math.sqrt(D / members)
    scaled = jnp.concatenate(split_two(factor_u.astype(F32) * scale[None, :]), axis=1)
    update = jnp.dot(scaled, v_twice, preferred_element_type=F32)
    return (mixed, fitness, update)


def solution(mesh):
    fine = Mesh(mesh.devices.reshape(Z, Y, X, C), ALL)
    return jax.shard_map(
        body,
        mesh=fine,
        in_specs=(
            P(ROW, COL),
            P(ROW, COL),
            P(COL, ROW),
            P(COL, ROW),
            P(ROW, COL),
            P(COL, None),
            P(None, ROW),
        ),
        out_specs=(P(ROW, COL), P(), P(COL, ROW)),
        check_vma=False,
    )
```

```python
import math

import jax
import jax.numpy as jnp
from jax import lax
from jax.experimental import pallas as pl
from jax.experimental.pallas import tpu as pltpu
from jax.sharding import Mesh
from jax.sharding import PartitionSpec as P

D = 5120
RANK = 4
SEQ = 64
SIGMA = 0.5
LANES = 128

Z, Y, X, C = 8, 4, 4, 2
ROW = ("z", "y")
COL = ("x", "core")
PLANE = ("y", "x", "core")
ALL = ("z", "y", "x", "core")
F32 = jnp.float32
BF16 = jnp.bfloat16


def shift(value, step):
    return lax.ppermute(value, "z", [(i, (i + step) % Z) for i in range(Z)])


def ring_gather(chunks):
    half = Z // 2
    blocks = [[chunk] + [None] * (Z - 1) for chunk in chunks]
    ends = [[chunk, chunk] for chunk in chunks]
    for step in range(1, half + 1):
        for k, end in enumerate(ends):
            if step < half or k % 2 == 0:
                end[0] = shift(end[0], 1)
                blocks[k][Z - step] = end[0]
            if step < half or k % 2 == 1:
                end[1] = shift(end[1], -1)
                blocks[k][step] = end[1]
    return blocks


def ring_scatter(chunks):
    half = Z // 2
    rows = chunks[0].shape[0] // Z
    ends = [{} for _ in chunks]
    for step in range(half, 0, -1):
        for k, chunk in enumerate(chunks):
            sends = {}
            for side, sign in ((0, 1), (1, -1)):
                if step == half and side != k % 2:
                    continue
                place = (sign * step) % Z
                block = chunk[place * rows : (place + 1) * rows]
                if sign in ends[k]:
                    block = block + ends[k][sign]
                else:
                    block = lax.optimization_barrier(block)
                sends[sign] = block.astype(BF16)
            sends = lax.optimization_barrier(sends)
            ends[k] = {sign: shift(value, sign).astype(F32) for sign, value in sends.items()}
    return [chunk[:rows] + end[1] + end[-1] for chunk, end in zip(chunks, ends)]


def layer_kernel(count, steps, units, *refs):
    blocks, (w_ref, corr_ref, *outs, acc, down, hidden) = refs[:count], refs[count:]
    step = pl.program_id(0)
    skip = units // LANES * LANES

    @pl.when(step < steps)
    def _():
        down[step] = w_ref[:, :units]
        rows = jnp.concatenate([block[...] for block in blocks], axis=0)
        part = jnp.dot(rows, w_ref[:, skip:], preferred_element_type=F32)

        @pl.when(step == 0)
        def _():
            acc[...] = part

        @pl.when(step > 0)
        def _():
            acc[...] += part

    @pl.when(step == steps - 1)
    def _():
        both = acc[...]
        gate = both[:, units - skip : 2 * units - skip]
        up = both[:, 2 * units - skip :] + SIGMA * corr_ref[...]
        hidden[...] = (gate / (1.0 + jnp.exp(-gate)) * up).astype(BF16)

    @pl.when(step >= steps)
    def _():
        out = lax.dot_general(
            hidden[...], down[step - steps], (((1,), (1,)), ((), ())), preferred_element_type=F32
        )
        rows = out.shape[0] // len(outs)
        for k, ref in enumerate(outs):
            ref[...] = out[k * rows : (k + 1) * rows]


def layer(blocks, weights, corr, steps):
    count = len(blocks)
    rows, units = corr.shape
    model, wide = weights.shape
    feat = model // steps
    small = blocks[0].shape[0]
    skip = units // LANES * LANES
    return pl.pallas_call(
        lambda *refs: layer_kernel(count, steps, units, *refs),
        grid=(2 * steps,),
        in_specs=[pl.BlockSpec((small, feat), lambda i: (0, jnp.minimum(i, steps - 1)))] * count
        + [
            pl.BlockSpec((feat, wide), lambda i: (jnp.minimum(i, steps - 1), 0)),
            pl.BlockSpec((rows, units), lambda i: (0, 0)),
        ],
        out_specs=[pl.BlockSpec((rows // 2, feat), lambda i: (0, jnp.maximum(i - steps, 0)))] * 2,
        out_shape=[jax.ShapeDtypeStruct((rows // 2, model), F32)] * 2,
        scratch_shapes=[
            pltpu.VMEM((rows, wide - skip), F32),
            pltpu.VMEM((steps, feat, units), BF16),
            pltpu.VMEM((rows, units), BF16),
        ],
        compiler_params=pltpu.CompilerParams(
            dimension_semantics=("arbitrary",), vmem_limit_bytes=40 * 1024 * 1024
        ),
        cost_estimate=pl.CostEstimate(
            flops=2 * rows * model * wide,
            bytes_accessed=2 * model * (wide + rows) + 4 * rows * model,
            transcendentals=rows * units,
        ),
    )(*blocks, weights, corr)


def split_two(value):
    high = value.astype(BF16)
    return high, (value - high.astype(F32)).astype(BF16)


def split_three(value):
    high = value.astype(BF16)
    return (high,) + split_two(value - high.astype(F32))


def body(tokens, target, w_gate, w_up, w_down, factor_u, factor_v):
    dev_rows, dev_feat = tokens.shape
    members = factor_u.shape[1] // RANK
    units = w_up.shape[1]
    cols = X * C
    model = dev_feat * cols
    own = dev_rows // cols
    local = dev_rows // SEQ
    z, y = lax.axis_index("z"), lax.axis_index("y")
    x, core = lax.axis_index("x"), lax.axis_index("core")

    packed = jnp.concatenate([w_down.T, w_gate, w_up], axis=1)
    v_twice = jnp.concatenate([factor_v, factor_v], axis=0)

    first = (z * Y + y) * local * RANK
    u_own = lax.dynamic_slice(factor_u, (0, first), (dev_feat, local * RANK))
    low = jnp.dot(tokens, u_own, preferred_element_type=F32)
    low = low.reshape(local, SEQ, local, RANK)
    low = jnp.concatenate([low[m, :, m] for m in range(local)], axis=0)
    extra = jnp.concatenate(split_two(low), axis=1)
    extra = jnp.pad(extra, ((0, 0), (0, LANES - extra.shape[1])))
    wide = jnp.concatenate([tokens, extra], axis=1).reshape(1, cols, own, dev_feat + LANES)
    wide = jnp.broadcast_to(wide, (Y, cols, own, dev_feat + LANES))
    packed, wide = lax.optimization_barrier((packed, wide))
    weights = lax.all_gather(packed, COL, axis=0, tiled=True)
    moved = lax.all_to_all(wide.reshape(Y * cols, own, dev_feat + LANES), PLANE, 0, 0, tiled=True)
    target, moved = lax.optimization_barrier((target, moved))
    goal = jnp.broadcast_to(target.reshape(1, cols, own, dev_feat), (Y, cols, own, dev_feat))
    goal = lax.all_to_all(goal.reshape(Y * cols, own, dev_feat), PLANE, 0, 0, tiled=True)
    goal = jnp.swapaxes(goal.reshape(Y, cols, own, dev_feat), 1, 2).reshape(Y, own, model)
    moved = moved.reshape(Y, cols, own, dev_feat + LANES)
    part = moved[..., dev_feat:].astype(F32)
    part = part[..., :RANK] + part[..., RANK : 2 * RANK]
    extra = jnp.concatenate(split_two(jnp.sum(part, axis=1)), axis=-1)
    extra = jnp.pad(extra, ((0, 0), (0, 0), (0, LANES - extra.shape[-1])))
    rows = jnp.swapaxes(moved[..., :dev_feat], 1, 2).reshape(Y, own, model)
    rows = jnp.concatenate([rows, extra], axis=2).reshape(Y * own, model + LANES)
    plane = Y * own
    mid = plane // 2

    first, second = ring_gather([rows[:mid], rows[mid:]])
    blocks = first + second

    row = lax.broadcasted_iota(jnp.int32, (Z * plane, members * RANK * 2), 0)
    column = lax.broadcasted_iota(jnp.int32, (Z * plane, members * RANK * 2), 1)
    row_y = row // (Z * mid) * (Y // 2) + row % mid // own
    row_z = (z + row // mid) % Z
    member = (row_z * Y + row_y) * local + (x * C + core) * own // SEQ
    spread_row = lax.broadcasted_iota(jnp.int32, (LANES, members * RANK * 2), 0)
    spread_col = lax.broadcasted_iota(jnp.int32, (LANES, members * RANK * 2), 1)
    spread = spread_col // (members * RANK) * RANK + spread_col % RANK == spread_row
    low = jnp.dot(
        jnp.concatenate([block[:, model:] for block in blocks], axis=0),
        spread.astype(BF16),
        preferred_element_type=F32,
    )
    low = jnp.where(column % (members * RANK) // RANK == member, low, 0.0).astype(BF16)
    corr = jnp.dot(low, v_twice, preferred_element_type=F32)

    sums = ring_scatter(layer(blocks, weights, corr, cols))
    total = jnp.concatenate(sums, axis=0).reshape(Y, own, model)
    score = jnp.sum(total * goal.astype(F32), axis=(1, 2)) / math.sqrt(SEQ * D)
    score = jnp.concatenate(split_three(score))
    score = jnp.broadcast_to(jnp.pad(score, (0, LANES - score.shape[0])), (Y * cols, own, LANES))

    back = jnp.swapaxes(total.astype(BF16).reshape(Y, own, cols, dev_feat), 1, 2)
    back = jnp.concatenate([back.reshape(Y * cols, own, dev_feat), score], axis=2)
    back = lax.all_to_all(back, PLANE, 0, 0, tiled=True)
    mixed = jnp.sum(back[..., :dev_feat].reshape(Y, dev_rows, dev_feat).astype(F32), axis=0)
    mixed = mixed.astype(BF16)

    score = back[:, 0, dev_feat : dev_feat + 3 * Y].astype(F32).reshape(Y, local, cols // local, 3, Y)
    score = (score[..., 2, :] + score[..., 1, :]) + score[..., 0, :]
    score = jnp.sum(score, axis=(0, 2)).T.reshape(Y * local)
    score = jnp.broadcast_to(jnp.pad(score, (0, LANES - Y * local)), (Z, 1, LANES))
    score = lax.all_to_all(score, "z", 0, 0, tiled=True)
    fitness = score[:, 0, : Y * local].reshape(members)

    scale = jnp.repeat(fitness, RANK) * math.sqrt(D / members)
    scaled = jnp.concatenate(split_two(factor_u.astype(F32) * scale[None, :]), axis=1)
    update = jnp.dot(scaled, v_twice, preferred_element_type=F32)
    return (mixed, fitness, update)


def solution(mesh):
    fine = Mesh(mesh.devices.reshape(Z, Y, X, C), ALL)
    return jax.shard_map(
        body,
        mesh=fine,
        in_specs=(
            P(ROW, COL),
            P(ROW, COL),
            P(COL, ROW),
            P(COL, ROW),
            P(ROW, COL),
            P(COL, None),
            P(None, ROW),
        ),
        out_specs=(P(ROW, COL), P(), P(COL, ROW)),
        check_vma=False,
    )
```

```python
import math

import jax
import jax.numpy as jnp
from jax import lax
from jax.sharding import Mesh
from jax.sharding import PartitionSpec as P

D = 5120
RANK = 4
SEQ = 64
SIGMA = 0.5
LANES = 128

Z, Y, X, C = 8, 4, 4, 2
ROW = ("z", "y")
COL = ("x", "core")
PLANE = ("y", "x", "core")
ALL = ("z", "y", "x", "core")
F32 = jnp.float32
BF16 = jnp.bfloat16


def shift(value, step):
    return lax.ppermute(value, "z", [(i, (i + step) % Z) for i in range(Z)])


def ring_gather(chunks):
    half = Z // 2
    rows, width = chunks[0].shape
    total = jnp.zeros((len(chunks) * Z * rows, width), chunks[0].dtype)
    ends = [[chunk, chunk] for chunk in chunks]
    landed = [(k, 0, chunk) for k, chunk in enumerate(chunks)]
    for step in range(1, half + 1):
        for k, end in enumerate(ends):
            if step < half or k % 2 == 0:
                end[0] = shift(end[0], 1)
                landed.append((k, Z - step, end[0]))
            if step < half or k % 2 == 1:
                end[1] = shift(end[1], -1)
                landed.append((k, step, end[1]))
    for k, place, block in landed:
        total = lax.dynamic_update_slice(total, block, ((k * Z + place) * rows, 0))
    return total


def ring_scatter(chunks):
    half = Z // 2
    rows = chunks[0].shape[0] // Z
    ends = [{} for _ in chunks]
    for step in range(half, 0, -1):
        for k, chunk in enumerate(chunks):
            sends = {}
            for side, sign in ((0, 1), (1, -1)):
                if step == half and side != k % 2:
                    continue
                place = (sign * step) % Z
                block = chunk[place * rows : (place + 1) * rows]
                if sign in ends[k]:
                    block = block + ends[k][sign]
                else:
                    block = lax.optimization_barrier(block)
                sends[sign] = block.astype(BF16)
            sends = lax.optimization_barrier(sends)
            ends[k] = {sign: shift(value, sign).astype(F32) for sign, value in sends.items()}
    return [chunk[:rows] + end[1] + end[-1] for chunk, end in zip(chunks, ends)]


def split_two(value):
    high = value.astype(BF16)
    return high, (value - high.astype(F32)).astype(BF16)


def split_three(value):
    high = value.astype(BF16)
    return (high,) + split_two(value - high.astype(F32))


def body(tokens, target, w_gate, w_up, w_down, factor_u, factor_v):
    dev_rows, dev_feat = tokens.shape
    members = factor_u.shape[1] // RANK
    units = w_up.shape[1]
    cols = X * C
    model = dev_feat * cols
    own = dev_rows // cols
    local = dev_rows // SEQ
    z, y = lax.axis_index("z"), lax.axis_index("y")
    x, core = lax.axis_index("x"), lax.axis_index("core")

    packed = jnp.concatenate([w_down.T, w_gate, w_up], axis=1)
    v_twice = jnp.concatenate([factor_v, factor_v], axis=0)

    first = (z * Y + y) * local * RANK
    u_own = lax.dynamic_slice(factor_u, (0, first), (dev_feat, local * RANK))
    low = jnp.dot(tokens, u_own, preferred_element_type=F32)
    low = low.reshape(local, SEQ, local, RANK)
    low = jnp.concatenate([low[m, :, m] for m in range(local)], axis=0)
    extra = jnp.concatenate(split_two(low), axis=1)
    extra = jnp.pad(extra, ((0, 0), (0, LANES - extra.shape[1])))
    wide = jnp.concatenate([tokens, extra], axis=1).reshape(1, cols, own, dev_feat + LANES)
    wide = jnp.broadcast_to(wide, (Y, cols, own, dev_feat + LANES))
    packed, wide = lax.optimization_barrier((packed, wide))
    weights = lax.all_gather(packed, COL, axis=0, tiled=True)
    moved = lax.all_to_all(wide.reshape(Y * cols, own, dev_feat + LANES), PLANE, 0, 0, tiled=True)
    moved = moved.reshape(Y, cols, own, dev_feat + LANES)
    part = moved[..., dev_feat:].astype(F32)
    part = part[..., :RANK] + part[..., RANK : 2 * RANK]
    extra = jnp.concatenate(split_two(jnp.sum(part, axis=1)), axis=-1)
    extra = jnp.pad(extra, ((0, 0), (0, 0), (0, LANES - extra.shape[-1])))
    rows = jnp.swapaxes(moved[..., :dev_feat], 1, 2).reshape(Y, own, model)
    rows = jnp.concatenate([rows, extra], axis=2).reshape(Y * own, model + LANES)
    plane = Y * own
    mid = plane // 2

    every = ring_gather([rows[:mid], rows[mid:]])

    row = lax.broadcasted_iota(jnp.int32, (Z * plane, members * RANK * 2), 0)
    column = lax.broadcasted_iota(jnp.int32, (Z * plane, members * RANK * 2), 1)
    row_y = row // (Z * mid) * (Y // 2) + row % mid // own
    row_z = (z + row // mid) % Z
    member = (row_z * Y + row_y) * local + (x * C + core) * own // SEQ
    spread_row = lax.broadcasted_iota(jnp.int32, (LANES, members * RANK * 2), 0)
    spread_col = lax.broadcasted_iota(jnp.int32, (LANES, members * RANK * 2), 1)
    spread = spread_col // (members * RANK) * RANK + spread_col % RANK == spread_row
    low = jnp.dot(
        every[:, model:],
        spread.astype(BF16),
        preferred_element_type=F32,
    )
    low = jnp.where(column % (members * RANK) // RANK == member, low, 0.0).astype(BF16)
    corr = jnp.dot(low, v_twice, preferred_element_type=F32)

    skip = units // LANES * LANES
    both = jnp.dot(every[:, :model], weights[:, skip:], preferred_element_type=F32)
    gate = both[:, units - skip : 2 * units - skip]
    up = both[:, 2 * units - skip :] + SIGMA * corr
    hidden = (jax.nn.silu(gate) * up).astype(BF16)
    hidden, target = lax.optimization_barrier((hidden, target))
    goal = jnp.broadcast_to(target.reshape(1, cols, own, dev_feat), (Y, cols, own, dev_feat))
    goal = lax.all_to_all(goal.reshape(Y * cols, own, dev_feat), PLANE, 0, 0, tiled=True)
    goal = jnp.swapaxes(goal.reshape(Y, cols, own, dev_feat), 1, 2).reshape(Y, own, model)
    outs = [
        lax.dot_general(
            part, weights[:, :units], (((1,), (1,)), ((), ())), preferred_element_type=F32
        )
        for part in (hidden[: Z * mid], hidden[Z * mid :])
    ]
    sums = ring_scatter(outs)
    total = jnp.concatenate(sums, axis=0).reshape(Y, own, model)
    score = jnp.sum(total * goal.astype(F32), axis=(1, 2)) / math.sqrt(SEQ * D)
    score = jnp.concatenate(split_three(score))
    score = jnp.broadcast_to(jnp.pad(score, (0, LANES - score.shape[0])), (Y * cols, own, LANES))

    back = jnp.swapaxes(total.astype(BF16).reshape(Y, own, cols, dev_feat), 1, 2)
    back = jnp.concatenate([back.reshape(Y * cols, own, dev_feat), score], axis=2)
    back = lax.all_to_all(back, PLANE, 0, 0, tiled=True)
    mixed = jnp.sum(back[..., :dev_feat].reshape(Y, dev_rows, dev_feat).astype(F32), axis=0)
    mixed = mixed.astype(BF16)

    score = back[:, 0, dev_feat : dev_feat + 3 * Y].astype(F32).reshape(Y, local, cols // local, 3, Y)
    score = (score[..., 2, :] + score[..., 1, :]) + score[..., 0, :]
    score = jnp.sum(score, axis=(0, 2)).T.reshape(Y * local)
    score = jnp.broadcast_to(jnp.pad(score, (0, LANES - Y * local)), (Z, 1, LANES))
    score = lax.all_to_all(score, "z", 0, 0, tiled=True)
    fitness = score[:, 0, : Y * local].reshape(members)

    scale = jnp.repeat(fitness, RANK) * math.sqrt(D / members)
    scaled = jnp.concatenate(split_two(factor_u.astype(F32) * scale[None, :]), axis=1)
    update = jnp.dot(scaled, v_twice, preferred_element_type=F32)
    return (mixed, fitness, update)


def solution(mesh):
    fine = Mesh(mesh.devices.reshape(Z, Y, X, C), ALL)
    return jax.shard_map(
        body,
        mesh=fine,
        in_specs=(
            P(ROW, COL),
            P(ROW, COL),
            P(COL, ROW),
            P(COL, ROW),
            P(ROW, COL),
            P(COL, None),
            P(None, ROW),
        ),
        out_specs=(P(ROW, COL), P(), P(COL, ROW)),
        check_vma=False,
    )
```

```python
import math

import jax
import jax.numpy as jnp
from jax import lax
from jax.sharding import Mesh
from jax.sharding import PartitionSpec as P

D = 5120
RANK = 4
SEQ = 64
SIGMA = 0.5
LANES = 128

Z, Y, X, C = 8, 4, 4, 2
ROW = ("z", "y")
COL = ("x", "core")
PLANE = ("y", "x", "core")
WALL = ("z", "x", "core")
ALL = ("z", "y", "x", "core")
F32 = jnp.float32
BF16 = jnp.bfloat16


def shift(value, step, axis="z"):
    n = {"z": Z, "y": Y}[axis]
    return lax.ppermute(value, axis, [(i, (i + step) % n) for i in range(n)])


def ring_gather(chunks):
    half = Z // 2
    rows, width = chunks[0].shape
    total = jnp.zeros((len(chunks) * Z * rows, width), chunks[0].dtype)
    ends = [[chunk, chunk] for chunk in chunks]
    landed = [(k, 0, chunk) for k, chunk in enumerate(chunks)]
    for step in range(1, half + 1):
        for k, end in enumerate(ends):
            if step < half or k % 2 == 0:
                end[0] = shift(end[0], 1)
                landed.append((k, Z - step, end[0]))
            if step < half or k % 2 == 1:
                end[1] = shift(end[1], -1)
                landed.append((k, step, end[1]))
    for k, place, block in landed:
        total = lax.dynamic_update_slice(total, block, ((k * Z + place) * rows, 0))
    return total


def ring_scatter(value, axis, n):
    half = n // 2
    rows = value.shape[0] // n
    mid = value.shape[1] // 2

    def block(distance):
        place = distance % n * rows
        return value[place : place + rows]

    sends = lax.optimization_barrier((block(half)[:, :mid], block(half)[:, mid:]))
    sends = [send.astype(BF16) for send in sends]
    ahead, behind = shift(sends[0], 1, axis), shift(sends[1], -1, axis)
    for step in range(half - 1, 0, -1):
        if step == half - 1:
            ahead = jnp.pad(ahead.astype(F32), ((0, 0), (0, mid)))
            behind = jnp.pad(behind.astype(F32), ((0, 0), (mid, 0)))
        sends = (
            (block(step) + ahead.astype(F32)).astype(BF16),
            (block(-step) + behind.astype(F32)).astype(BF16),
        )
        sends = lax.optimization_barrier(sends)
        ahead, behind = shift(sends[0], 1, axis), shift(sends[1], -1, axis)
    return block(0) + ahead.astype(F32) + behind.astype(F32)


def turn(value, start):
    size = value.shape[0]
    return lax.dynamic_slice_in_dim(jnp.concatenate([value, value], axis=0), start, size, axis=0)


def split_two(value):
    high = value.astype(BF16)
    return high, (value - high.astype(F32)).astype(BF16)


def split_three(value):
    high = value.astype(BF16)
    return (high,) + split_two(value - high.astype(F32))


def body(tokens, target, w_gate, w_up, w_down, factor_u, factor_v):
    dev_rows, dev_feat = tokens.shape
    members = factor_u.shape[1] // RANK
    units = w_up.shape[1]
    cols = X * C
    model = dev_feat * cols
    own = dev_rows // cols
    local = dev_rows // SEQ
    z, y = lax.axis_index("z"), lax.axis_index("y")
    x, core = lax.axis_index("x"), lax.axis_index("core")

    packed = jnp.concatenate([w_down.T, w_gate, w_up], axis=1)
    v_twice = jnp.concatenate([factor_v, factor_v], axis=0)

    first = (z * Y + y) * local * RANK
    u_own = lax.dynamic_slice(factor_u, (0, first), (dev_feat, local * RANK))
    low = jnp.dot(tokens, u_own, preferred_element_type=F32)
    low = low.reshape(local, SEQ, local, RANK)
    low = jnp.concatenate([low[m, :, m] for m in range(local)], axis=0)
    extra = jnp.concatenate(split_two(low), axis=1)
    extra = jnp.pad(extra, ((0, 0), (0, LANES - extra.shape[1])))
    wide = jnp.concatenate([tokens, extra], axis=1).reshape(1, cols, own, dev_feat + LANES)
    wide = jnp.broadcast_to(wide, (Y, cols, own, dev_feat + LANES))
    packed, wide = lax.optimization_barrier((packed, wide))
    weights = lax.all_gather(packed, COL, axis=0, tiled=True)
    moved = lax.all_to_all(wide.reshape(Y * cols, own, dev_feat + LANES), PLANE, 0, 0, tiled=True)
    target, moved = lax.optimization_barrier((target, moved))
    part = own // 2
    aims = target.reshape(cols, 2, part, dev_feat)
    goal = jnp.broadcast_to(aims[:, 0], (Y, cols, part, dev_feat)).reshape(Y * cols, part, dev_feat)
    goal = lax.all_to_all(goal, PLANE, 0, 0, tiled=True)
    goal = jnp.swapaxes(goal.reshape(Y, cols, part, dev_feat), 1, 2).reshape(Y, part, model)
    moved = moved.reshape(Y, cols, own, dev_feat + LANES)
    low = moved[..., dev_feat:].astype(F32)
    low = low[..., :RANK] + low[..., RANK : 2 * RANK]
    extra = jnp.concatenate(split_two(jnp.sum(low, axis=1)), axis=-1)
    extra = jnp.pad(extra, ((0, 0), (0, 0), (0, LANES - extra.shape[-1])))
    rows = jnp.swapaxes(moved[..., :dev_feat], 1, 2).reshape(Y, own, model)
    rows = jnp.concatenate([rows, extra], axis=2).reshape(Y * own, model + LANES)
    plane = Y * own
    mid = plane // 2

    every = ring_gather([rows[:mid], rows[mid:]])

    row = lax.broadcasted_iota(jnp.int32, (Z * plane, members * RANK * 2), 0)
    column = lax.broadcasted_iota(jnp.int32, (Z * plane, members * RANK * 2), 1)
    row_y = row // (Z * mid) * (Y // 2) + row % mid // own
    row_z = (z + row // mid) % Z
    member = (row_z * Y + row_y) * local + (x * C + core) * own // SEQ
    spread_row = lax.broadcasted_iota(jnp.int32, (LANES, members * RANK * 2), 0)
    spread_col = lax.broadcasted_iota(jnp.int32, (LANES, members * RANK * 2), 1)
    spread = spread_col // (members * RANK) * RANK + spread_col % RANK == spread_row
    low = jnp.dot(
        every[:, model:],
        spread.astype(BF16),
        preferred_element_type=F32,
    )
    low = jnp.where(column % (members * RANK) // RANK == member, low, 0.0).astype(BF16)
    corr = jnp.dot(low, v_twice, preferred_element_type=F32)

    skip = units // LANES * LANES
    both = jnp.dot(every[:, :model], weights[:, skip:], preferred_element_type=F32)
    gate = both[:, units - skip : 2 * units - skip]
    up = both[:, 2 * units - skip :] + SIGMA * corr
    hidden = (jax.nn.silu(gate) * up).astype(BF16)
    hidden, goal = lax.optimization_barrier((hidden, goal))

    hidden = hidden.reshape(2, Z, Y // 2, 2, part, units)
    first = jnp.transpose(hidden[:, :, :, 0], (1, 0, 2, 3, 4)).reshape(Z * Y * part, units)
    second = jnp.transpose(hidden[:, :, :, 1], (1, 0, 2, 3, 4)).reshape(Z, Y, part, units)
    second = jnp.swapaxes(turn(second, (Z - z) % Z), 0, 1)
    second = turn(second, y).reshape(Y * Z * part, units)
    down = weights[:, :units]

    def project(rows_of):
        return lax.dot_general(rows_of, down, (((1,), (1,)), ((), ())), preferred_element_type=F32)

    def leave(total, devices):
        out = total.astype(BF16).reshape(devices, part, cols, dev_feat)
        return jnp.swapaxes(out, 1, 2).reshape(devices * cols, part, dev_feat)

    second = ring_scatter(project(second), "y", Y)
    second = lax.all_to_all(leave(second, Z), WALL, 0, 0, tiled=True)
    second = jnp.sum(second.reshape(Z, cols, part, dev_feat).astype(F32), axis=0)
    late = jnp.sum((second * aims[:, 1].astype(F32)).reshape(local, -1), axis=1)

    first = ring_scatter(project(first), "z", Z)
    early = jnp.sum(first.reshape(Y, part, model) * goal.astype(F32), axis=(1, 2))
    score = jnp.concatenate([early, late]) / math.sqrt(SEQ * D)
    count = Y + local
    score = jnp.concatenate(split_three(score))
    score = jnp.broadcast_to(jnp.pad(score, (0, LANES - 3 * count)), (Y * cols, part, LANES))
    back = jnp.concatenate([leave(first, Y), score], axis=2)
    back = lax.all_to_all(back, PLANE, 0, 0, tiled=True)
    first = jnp.sum(back[..., :dev_feat].reshape(Y, cols, part, dev_feat).astype(F32), axis=0)
    mixed = jnp.stack([first, second], axis=1).astype(BF16).reshape(dev_rows, dev_feat)

    score = back[:, 0, dev_feat : dev_feat + 3 * count].astype(F32).reshape(Y, cols, 3, count)
    score = (score[:, :, 2] + score[:, :, 1]) + score[:, :, 0]
    early = score[..., :Y].reshape(Y, local, cols // local, Y)
    score = jnp.sum(early, axis=(0, 2)).T + jnp.sum(score[..., Y:], axis=1)
    score = score.reshape(Y * local)
    score = jnp.broadcast_to(jnp.pad(score, (0, LANES - Y * local)), (Z, 1, LANES))
    score = lax.all_to_all(score, "z", 0, 0, tiled=True)
    fitness = score[:, 0, : Y * local].reshape(members)

    scale = jnp.repeat(fitness, RANK) * math.sqrt(D / members)
    scaled = jnp.concatenate(split_two(factor_u.astype(F32) * scale[None, :]), axis=1)
    update = jnp.dot(scaled, v_twice, preferred_element_type=F32)
    return (mixed, fitness, update)


def solution(mesh):
    fine = Mesh(mesh.devices.reshape(Z, Y, X, C), ALL)
    return jax.shard_map(
        body,
        mesh=fine,
        in_specs=(
            P(ROW, COL),
            P(ROW, COL),
            P(COL, ROW),
            P(COL, ROW),
            P(ROW, COL),
            P(COL, None),
            P(None, ROW),
        ),
        out_specs=(P(ROW, COL), P(), P(COL, ROW)),
        check_vma=False,
    )
```

```python
import math

import jax
import jax.numpy as jnp
from jax import lax
from jax.sharding import Mesh
from jax.sharding import PartitionSpec as P

D = 5120
RANK = 4
SEQ = 64
SIGMA = 0.5
LANES = 128

Z, Y, X, C = 8, 4, 4, 2
ROW = ("z", "y")
COL = ("x", "core")
PLANE = ("y", "x", "core")
WALL = ("z", "x", "core")
ALL = ("z", "y", "x", "core")
F32 = jnp.float32
BF16 = jnp.bfloat16


def shift(value, step, axis="z"):
    n = {"z": Z, "y": Y}[axis]
    return lax.ppermute(value, axis, [(i, (i + step) % n) for i in range(n)])


def ring_gather(value):
    half = Z // 2
    rows, width = value.shape
    mid = width // LANES // 2 * LANES
    total = jnp.zeros((Z * rows, width), value.dtype)
    ahead = behind = value
    landed = [(0, 0, value)]
    for step in range(1, half):
        ahead, behind = shift(ahead, 1), shift(behind, -1)
        landed += [(Z - step, 0, ahead), (step, 0, behind)]
    landed.append((half, 0, shift(ahead[:, :mid], 1)))
    landed.append((half, mid, shift(behind[:, mid:], -1)))
    for place, column, block in landed:
        total = lax.dynamic_update_slice(total, block, (place * rows, column))
    return total


def ring_scatter(value, axis, n):
    half = n // 2
    rows = value.shape[0] // n
    mid = value.shape[1] // 2

    def block(distance):
        place = distance % n * rows
        return value[place : place + rows]

    sends = lax.optimization_barrier((block(half)[:, :mid], block(half)[:, mid:]))
    sends = [send.astype(BF16) for send in sends]
    ahead, behind = shift(sends[0], 1, axis), shift(sends[1], -1, axis)
    for step in range(half - 1, 0, -1):
        if step == half - 1:
            ahead = jnp.pad(ahead.astype(F32), ((0, 0), (0, mid)))
            behind = jnp.pad(behind.astype(F32), ((0, 0), (mid, 0)))
        sends = (
            (block(step) + ahead.astype(F32)).astype(BF16),
            (block(-step) + behind.astype(F32)).astype(BF16),
        )
        sends = lax.optimization_barrier(sends)
        ahead, behind = shift(sends[0], 1, axis), shift(sends[1], -1, axis)
    return block(0) + ahead.astype(F32) + behind.astype(F32)


def turn(value, start):
    size = value.shape[0]
    return lax.dynamic_slice_in_dim(jnp.concatenate([value, value], axis=0), start, size, axis=0)


def split_two(value):
    high = value.astype(BF16)
    return high, (value - high.astype(F32)).astype(BF16)


def split_three(value):
    high = value.astype(BF16)
    return (high,) + split_two(value - high.astype(F32))


def body(tokens, target, w_gate, w_up, w_down, factor_u, factor_v):
    dev_rows, dev_feat = tokens.shape
    members = factor_u.shape[1] // RANK
    units = w_up.shape[1]
    cols = X * C
    model = dev_feat * cols
    own = dev_rows // cols
    local = dev_rows // SEQ
    z, y = lax.axis_index("z"), lax.axis_index("y")
    x, core = lax.axis_index("x"), lax.axis_index("core")

    packed = jnp.concatenate([w_down.T, w_gate, w_up], axis=1)
    v_twice = jnp.concatenate([factor_v, factor_v], axis=0)

    first = (z * Y + y) * local * RANK
    u_own = lax.dynamic_slice(factor_u, (0, first), (dev_feat, local * RANK))
    low = jnp.dot(tokens, u_own, preferred_element_type=F32)
    low = low.reshape(local, SEQ, local, RANK)
    low = jnp.concatenate([low[m, :, m] for m in range(local)], axis=0)
    extra = jnp.concatenate(split_two(low), axis=1)
    extra = jnp.pad(extra, ((0, 0), (0, LANES - extra.shape[1])))
    wide = jnp.concatenate([tokens, extra], axis=1).reshape(1, cols, own, dev_feat + LANES)
    wide = jnp.broadcast_to(wide, (Y, cols, own, dev_feat + LANES))
    packed, wide = lax.optimization_barrier((packed, wide))
    weights = lax.all_gather(packed, COL, axis=0, tiled=True)
    moved = lax.all_to_all(wide.reshape(Y * cols, own, dev_feat + LANES), PLANE, 0, 0, tiled=True)
    target, moved = lax.optimization_barrier((target, moved))
    part = own // 2
    aims = target.reshape(cols, 2, part, dev_feat)
    goal = jnp.broadcast_to(aims[:, 0], (Y, cols, part, dev_feat)).reshape(Y * cols, part, dev_feat)
    goal = lax.all_to_all(goal, PLANE, 0, 0, tiled=True)
    goal = jnp.swapaxes(goal.reshape(Y, cols, part, dev_feat), 1, 2).reshape(Y, part, model)
    moved = moved.reshape(Y, cols, own, dev_feat + LANES)
    low = moved[..., dev_feat:].astype(F32)
    low = low[..., :RANK] + low[..., RANK : 2 * RANK]
    extra = jnp.concatenate(split_two(jnp.sum(low, axis=1)), axis=-1)
    extra = jnp.pad(extra, ((0, 0), (0, 0), (0, LANES - extra.shape[-1])))
    rows = jnp.swapaxes(moved[..., :dev_feat], 1, 2).reshape(Y, own, model)
    rows = jnp.concatenate([rows, extra], axis=2).reshape(Y * own, model + LANES)
    plane = Y * own

    every = ring_gather(rows)

    row = lax.broadcasted_iota(jnp.int32, (Z * plane, members * RANK * 2), 0)
    column = lax.broadcasted_iota(jnp.int32, (Z * plane, members * RANK * 2), 1)
    row_y = row % plane // own
    row_z = (z + row // plane) % Z
    member = (row_z * Y + row_y) * local + (x * C + core) * own // SEQ
    spread_row = lax.broadcasted_iota(jnp.int32, (LANES, members * RANK * 2), 0)
    spread_col = lax.broadcasted_iota(jnp.int32, (LANES, members * RANK * 2), 1)
    spread = spread_col // (members * RANK) * RANK + spread_col % RANK == spread_row
    low = jnp.dot(
        every[:, model:],
        spread.astype(BF16),
        preferred_element_type=F32,
    )
    low = jnp.where(column % (members * RANK) // RANK == member, low, 0.0).astype(BF16)
    corr = jnp.dot(low, v_twice, preferred_element_type=F32)

    skip = units // LANES * LANES
    both = jnp.dot(every[:, :model], weights[:, skip:], preferred_element_type=F32)
    gate = both[:, units - skip : 2 * units - skip]
    up = both[:, 2 * units - skip :] + SIGMA * corr
    hidden = (jax.nn.silu(gate) * up).astype(BF16)
    hidden, goal = lax.optimization_barrier((hidden, goal))

    hidden = hidden.reshape(Z, Y, 2, part, units)
    first = hidden[:, :, 0].reshape(Z * Y * part, units)
    second = hidden[:, :, 1]
    second = jnp.swapaxes(turn(second, (Z - z) % Z), 0, 1)
    second = turn(second, y).reshape(Y * Z * part, units)
    down = weights[:, :units]

    def project(rows_of):
        return lax.dot_general(rows_of, down, (((1,), (1,)), ((), ())), preferred_element_type=F32)

    def leave(total, devices):
        out = total.astype(BF16).reshape(devices, part, cols, dev_feat)
        return jnp.swapaxes(out, 1, 2).reshape(devices * cols, part, dev_feat)

    second = ring_scatter(project(second), "y", Y)
    second = lax.all_to_all(leave(second, Z), WALL, 0, 0, tiled=True)
    second = jnp.sum(second.reshape(Z, cols, part, dev_feat).astype(F32), axis=0)
    late = jnp.sum((second * aims[:, 1].astype(F32)).reshape(local, -1), axis=1)

    first = ring_scatter(project(first), "z", Z)
    early = jnp.sum(first.reshape(Y, part, model) * goal.astype(F32), axis=(1, 2))
    score = jnp.concatenate([early, late]) / math.sqrt(SEQ * D)
    count = Y + local
    score = jnp.concatenate(split_three(score))
    score = jnp.broadcast_to(jnp.pad(score, (0, LANES - 3 * count)), (Y * cols, part, LANES))
    back = jnp.concatenate([leave(first, Y), score], axis=2)
    back = lax.all_to_all(back, PLANE, 0, 0, tiled=True)
    first = jnp.sum(back[..., :dev_feat].reshape(Y, cols, part, dev_feat).astype(F32), axis=0)
    mixed = jnp.stack([first, second], axis=1).astype(BF16).reshape(dev_rows, dev_feat)

    score = back[:, 0, dev_feat : dev_feat + 3 * count].astype(F32).reshape(Y, cols, 3, count)
    score = (score[:, :, 2] + score[:, :, 1]) + score[:, :, 0]
    early = score[..., :Y].reshape(Y, local, cols // local, Y)
    score = jnp.sum(early, axis=(0, 2)).T + jnp.sum(score[..., Y:], axis=1)
    score = score.reshape(Y * local)
    score = jnp.broadcast_to(jnp.pad(score, (0, LANES - Y * local)), (Z, 1, LANES))
    score = lax.all_to_all(score, "z", 0, 0, tiled=True)
    fitness = score[:, 0, : Y * local].reshape(members)

    scale = jnp.repeat(fitness, RANK) * math.sqrt(D / members)
    scaled = jnp.concatenate(split_two(factor_u.astype(F32) * scale[None, :]), axis=1)
    update = jnp.dot(scaled, v_twice, preferred_element_type=F32)
    return (mixed, fitness, update)


def solution(mesh):
    fine = Mesh(mesh.devices.reshape(Z, Y, X, C), ALL)
    return jax.shard_map(
        body,
        mesh=fine,
        in_specs=(
            P(ROW, COL),
            P(ROW, COL),
            P(COL, ROW),
            P(COL, ROW),
            P(ROW, COL),
            P(COL, None),
            P(None, ROW),
        ),
        out_specs=(P(ROW, COL), P(), P(COL, ROW)),
        check_vma=False,
    )
```
